512 devices in a mesh: chan: 64 (over x, z_lo, core), stn: 8 (over y, z_hi).
Axes of the slice: x: 4, y: 4, z: 16 (z_hi: 2, z_lo: 8; z = z_hi * 8 + z_lo), core: 2. Of those that a mesh axis runs over, the one named last changes fastest.
Arguments:
- voltages: bfloat16 [2, 512, 524288], P(None, 'stn', 'chan'), may hold values from -12 to 12
Outputs:
- visibilities: bfloat16 [2048, 512, 5, 128], P('chan', 'stn')
The draws below stay inside these ranges and needn't reach their ends.
All inputs are finite; a program needn't handle non-finite values.
Results may differ from the reference program's by a relative error of at most 0.0031.
Values may be sent and summed in bfloat16 or wider, within the bound.
A program may use at most 64 MiB of HBM per device.

```python
import math
import jax
import jax.numpy as jnp
from jax import lax

IN_DEV = 64
INPUTS = 512
NCH = 2048
TAPS = 4
SPECTRA = 256
SAMPLES = 524288
CH_DEV = 32
LAGS = 5
N_CHAN = 64
N_STN = 8


sky_count = 4


longest_delay = 64


def draw_voltages(key, part):
    key = jax.random.fold_in(key, 7)
    sky_key, gain_key, delay_key, noise_key = jax.random.split(key, 4)
    sky = jax.random.normal(sky_key, (sky_count, 2, SAMPLES + longest_delay), jnp.float32)
    gains = 0.4 * jax.random.normal(gain_key, (INPUTS, sky_count, 2), jnp.float32)
    noise = jax.random.normal(noise_key, (2, INPUTS, SAMPLES), jnp.float32)
    delays = jax.random.randint(delay_key, (INPUTS,), 0, longest_delay)

    def one_input(packed):
        delay_here, gain_here = packed
        window = lax.dynamic_slice_in_dim(sky, delay_here, SAMPLES, axis=2)
        real_part = jnp.sum(gain_here[:, 0, None] * window[:, 0] - gain_here[:, 1, None] * window[:, 1], axis=0)
        imag_part = jnp.sum(gain_here[:, 0, None] * window[:, 1] + gain_here[:, 1, None] * window[:, 0], axis=0)
        return jnp.stack([real_part, imag_part])
    signal = lax.map(one_input, (delays, gains))
    values = jnp.moveaxis(signal, 1, 0) + noise
    return jnp.clip(values, -12.0, 12.0).astype(jnp.bfloat16)


def setup_inputs(seed: int = 0) -> dict:
    splits = jax.random.split(jax.random.key(seed), 2)
    return {
        "voltages": draw_voltages(jax.random.fold_in(splits[1], 71), 0),
    }


def prototype(tap_count, chan_count):
    position = jnp.arange(tap_count * chan_count, dtype=jnp.float32) + 0.5
    centered = (position - tap_count * chan_count / 2.0) / chan_count
    window = 0.5 - 0.5 * jnp.cos(2.0 * math.pi * position / (tap_count * chan_count))
    return (jnp.sinc(centered) * window).reshape(tap_count, chan_count)


def reference(voltages):
    weights = prototype(TAPS, NCH)
    grouped = jnp.moveaxis(voltages.reshape(2, N_STN, IN_DEV, SAMPLES), 1, 0)

    def spectra_of(station_block):
        samples_f = station_block.astype(jnp.float32).reshape(2, IN_DEV, SPECTRA, NCH)
        padded = jnp.pad(samples_f, ((0, 0), (0, 0), (TAPS - 1, 0), (0, 0)))
        filtered = weights[0] * padded[:, :, 0:SPECTRA]
        for tap_index in range(1, TAPS):
            filtered = filtered + weights[tap_index] * padded[:, :, tap_index:tap_index + SPECTRA]
        spectrum = jnp.fft.fft(lax.complex(filtered[0], filtered[1]), axis=-1) * (NCH ** -0.5)
        return jnp.stack([jnp.real(spectrum), jnp.imag(spectrum)]).astype(jnp.bfloat16)

    channelized = lax.map(spectra_of, grouped)
    arranged = jnp.transpose(channelized, (3, 1, 0, 2, 4)).reshape(SPECTRA, 2, INPUTS, NCH)
    by_channel = jnp.moveaxis(arranged.reshape(SPECTRA, 2, INPUTS, N_CHAN, CH_DEV), 3, 0)

    def visibilities_of(chan_block):
        blocks = chan_block.astype(jnp.float32).reshape(SPECTRA, 2, N_STN, IN_DEV, CH_DEV)
        real_list = []
        imag_list = []
        for lag_index in range(LAGS):
            partner = jnp.roll(blocks, -lag_index, axis=2)
            products = jnp.einsum("sxbpc,sybqc->cbxpyq", blocks, partner,
                                  precision=lax.Precision.HIGHEST) * (1.0 / SPECTRA)
            real_list.append(products[:, :, 0, :, 0] + products[:, :, 1, :, 1])
            imag_list.append(products[:, :, 1, :, 0] - products[:, :, 0, :, 1])
        real_all = jnp.stack(real_list, axis=3).reshape(CH_DEV, INPUTS, LAGS, IN_DEV)
        imag_all = jnp.stack(imag_list, axis=3).reshape(CH_DEV, INPUTS, LAGS, IN_DEV)
        return jnp.concatenate([real_all, imag_all], axis=3).astype(jnp.bfloat16)

    result = lax.map(visibilities_of, by_channel)
    return result.reshape(NCH, INPUTS, LAGS, 2 * IN_DEV)
```

```python
import math

import jax
import jax.numpy as jnp
import numpy as np
from jax import lax
from jax.experimental import pallas as pl
from jax.experimental.pallas import tpu as pltpu
from jax.sharding import PartitionSpec as P

MESH = pl.DeviceIdType.MESH
NCH = 2048
TAPS = 4
SPEC = 4
RAD = 16
LEN = 128
IN_DEV = 64
NX, NZL, NCORE, NY, NZH = 4, 8, 2, 4, 2
NXC = NX * NCORE
PLANE = NXC * NY
NZ = NZL * NZH
CHAN = NX * NZL * NCORE
STN = NY * NZH
LAGS = STN // 2 + 1
KK = RAD // NY
CHUNKS = 2 * KK
BF = jnp.bfloat16
F32 = jnp.float32


def tables():
    position = np.arange(TAPS * NCH, dtype=np.float64) + 0.5
    centered = (position - TAPS * NCH / 2.0) / NCH
    window = 0.5 - 0.5 * np.cos(2.0 * math.pi * position / (TAPS * NCH))
    weights = (np.sinc(centered) * window).reshape(TAPS * RAD, LEN).astype(np.float32)
    angle = 2.0 * math.pi / NCH * np.outer(np.arange(RAD), np.arange(LEN))
    twiddle = np.concatenate([np.cos(angle), np.sin(angle)], axis=0).astype(np.float32)
    x, core, zl, half = np.meshgrid(
        np.arange(NX), np.arange(NCORE), np.arange(NZL), np.arange(2), indexing="ij"
    )
    order = (((x * NZL + zl) * NCORE + core) * 2 + half).reshape(-1)
    angle = 2.0 * math.pi / LEN * (np.outer(order, np.arange(LEN)) % LEN)
    table = np.concatenate([np.cos(angle), np.sin(angle)], axis=1) * NCH**-0.5
    high = table.astype(np.float32).astype(BF)
    low = (table - high.astype(np.float64)).astype(np.float32).astype(BF)
    swap = np.zeros((16, 16, 16, 16), np.float32)
    for t in range(16):
        for j in range(16):
            swap[j, t, t, j] = 1.0
    swap = swap.reshape(256, 256).astype(BF)
    return weights, twiddle, high, low, swap


def transform(points):
    count = len(points)
    if count == 1:
        return points
    even, odd = transform(points[0::2]), transform(points[1::2])
    low, high = [], []
    for k in range(count // 2):
        re, im = odd[k]
        if k == 0:
            pass
        elif 4 * k == count:
            re, im = im, -re
        elif 8 * k == count:
            re, im = (re + im) * math.sqrt(0.5), (im - re) * math.sqrt(0.5)
        elif 8 * k == 3 * count:
            re, im = (im - re) * math.sqrt(0.5), (re + im) * -math.sqrt(0.5)
        else:
            c, s = math.cos(2 * math.pi * k / count), math.sin(2 * math.pi * k / count)
            re, im = re * c + im * s, im * c - re * s
        low.append((even[k][0] + re, even[k][1] + im))
        high.append((even[k][0] - re, even[k][1] - im))
    return low + high


def kernel(
    x_ref, wts_ref, tw_ref, ah_ref, al_ref, swap_ref, out_ref,
    halo, yh, yl, b1, r1, zs, zr, gw, ob,
    halo_send, halo_recv, xy_send, xy_recv, z_send, z_recv, o_send, o_recv,
):
    chan, stn = lax.axis_index("chan"), lax.axis_index("stn")
    core = chan % NCORE
    zl = (chan // NCORE) % NZL
    x = chan // (NCORE * NZL)
    y, zh = stn // NZH, stn % NZH
    me_xy = y * NXC + x * NCORE + core
    me_z = zh * NZL + zl

    def at_xy(i):
        xc = i % NXC
        return {"chan": ((xc // NCORE) * NZL + zl) * NCORE + xc % NCORE, "stn": (i // NXC) * NZH + zh}

    def at_z(i):
        return {"chan": (x * NZL + i % NZL) * NCORE + core, "stn": y * NZH + i // NZL}

    after = {"chan": (chan + 1) % CHAN, "stn": stn}
    before = {"chan": (chan + CHAN - 1) % CHAN, "stn": stn}

    barrier = pltpu.get_barrier_semaphore()

    def greet(device):
        pl.semaphore_signal(barrier, inc=1, device_id=device, device_id_type=MESH)

    greet(after)
    greet(before)

    @pl.loop(1, PLANE)
    def _(j):
        greet(at_xy((me_xy + j) % PLANE))

    @pl.loop(1, NZ)
    def _(j):
        greet(at_z((me_z + j) % NZ))

    pl.semaphore_wait(barrier, PLANE + NZ)

    def send_halo(block, slot):
        pltpu.make_async_remote_copy(
            src_ref=x_ref.at[:, :, pl.ds(block * NCH, NCH)],
            dst_ref=halo.at[slot],
            send_sem=halo_send.at[slot],
            recv_sem=halo_recv.at[slot],
            device_id=after,
            device_id_type=MESH,
        ).start()

    def wait_halo(slot):
        pltpu.make_async_copy(halo.at[slot], halo.at[slot], halo_recv.at[slot]).wait()

    send_halo(3, 2)
    send_halo(2, 1)
    send_halo(1, 0)
    valid = (chan > 0).astype(F32)

    def spectrum(s):
        @pl.loop(0, IN_DEV // 16)
        def _(tile):
            rows = pl.ds(pl.multiple_of(tile * 16, 16), 16)
            points = []
            for a in range(RAD):
                pair = []
                for part in range(2):
                    here = there = None
                    for tap in range(TAPS):
                        w = wts_ref[pl.ds(tap * RAD + a, 1), :]
                        j = s - 3 + tap
                        if j >= 0:
                            v = x_ref[part, rows, pl.ds(j * NCH + a * LEN, LEN)].astype(F32) * w
                            here = v if here is None else here + v
                        else:
                            v = halo[3 + j, part, rows, pl.ds(a * LEN, LEN)].astype(F32) * w
                            there = v if there is None else there + v
                    pair.append(here if there is None else here + there * valid)
                points.append(tuple(pair))
            turned = transform(points)
            low_rows = pl.ds(pl.multiple_of(IN_DEV + tile * 16, 16), 16)
            for k in range(RAD):
                re, im = turned[k]
                if k > 0:
                    c, sn = tw_ref[pl.ds(k, 1), :], tw_ref[pl.ds(RAD + k, 1), :]
                    re, im = re * c + im * sn, im * c - re * sn
                re_h, im_h = re.astype(BF), im.astype(BF)
                re_l = (re - re_h.astype(F32)).astype(BF)
                im_l = (im - im_h.astype(F32)).astype(BF)
                for ref, r, i in ((yh, re_h, im_h), (yl, re_l, im_l)):
                    ref[s % 2, k, rows, 0:LEN] = r
                    ref[s % 2, k, rows, LEN : 2 * LEN] = i
                    ref[s % 2, k, low_rows, 0:LEN] = i
                    ref[s % 2, k, low_rows, LEN : 2 * LEN] = -r

    def dot_nt(a, b):
        return lax.dot_general(a, b, (((1,), (1,)), ((), ())), preferred_element_type=F32)

    def channels(chunk, kk):
        @pl.loop(0, NY)
        def _(yd):
            k = yd * KK + kk
            for s in range(2):
                high, low = yh[s, k], yl[s, k]
                o = dot_nt(ah_ref[...], high) + dot_nt(al_ref[...], high) + dot_nt(ah_ref[...], low)
                b1[chunk, pl.ds(yd * NXC, NXC), s] = o.astype(BF).reshape(NXC, 16, LEN)

        pltpu.make_async_copy(b1.at[chunk, me_xy], r1.at[chunk, me_xy], xy_recv.at[chunk]).start()

        @pl.loop(1, PLANE)
        def _(j):
            to = (me_xy + j) % PLANE
            pltpu.make_async_remote_copy(
                src_ref=b1.at[chunk, to],
                dst_ref=r1.at[chunk, me_xy],
                send_sem=xy_send,
                recv_sem=xy_recv.at[chunk],
                device_id=at_xy(to),
                device_id_type=MESH,
            ).start()

    def spread(chunk):
        pltpu.make_async_copy(r1.at[chunk], r1.at[chunk], xy_recv.at[chunk]).wait()

        @pl.loop(0, NY)
        def _(yd):
            rows = r1[chunk, pl.ds(yd * NXC, NXC)].reshape(256, LEN)
            o = jnp.dot(swap_ref[...], rows, preferred_element_type=F32).astype(BF)
            zs[chunk, :, :, yd] = o.reshape(NZL, 2, 16, LEN)

        pltpu.make_async_copy(zs.at[chunk, zl], zr.at[chunk, me_z], z_recv.at[chunk]).start()

        @pl.loop(1, NZ)
        def _(j):
            to = (me_z + j) % NZ
            pltpu.make_async_remote_copy(
                src_ref=zs.at[chunk, to % NZL],
                dst_ref=zr.at[chunk, me_z],
                send_sem=z_send,
                recv_sem=z_recv.at[chunk],
                device_id=at_z(to),
                device_id_type=MESH,
            ).start()

    def phase(base):
        channels(base, 0)

        @pl.loop(1, KK)
        def _(kk):
            channels(base + kk, kk)
            spread(base + kk - 1)

        spread(base + KK - 1)

    spectrum(3)
    wait_halo(2)
    spectrum(2)
    phase(0)
    wait_halo(1)
    spectrum(1)
    wait_halo(0)
    spectrum(0)
    phase(KK)

    lane = lax.broadcasted_iota(jnp.int32, (IN_DEV, LEN), 1)
    scale = 1.0 / (CHAN * SPEC)
    sign = jnp.where(lane < IN_DEV, scale, -scale).astype(F32)

    @pl.loop(0, KK)
    def _(kk):
        for base in (0, KK):
            pltpu.make_async_copy(zr.at[base + kk], zr.at[base + kk], z_recv.at[base + kk]).wait()

        @pl.loop(0, 2)
        def _(half):
            for g in range(STN + LAGS - 1):
                st = (zh + g) % STN
                for sp in range(2):
                    part = zr[sp * KK + kk, pl.ds((st % NZH) * NZL, NZL), half, st // NZH]
                    gw[pl.ds(sp * 128, 128), pl.ds(g * LEN, LEN)] = part.reshape(128, LEN)
            slot = half * KK + kk
            for yo in range(NY):
                own = gw[:, pl.ds(2 * yo * LEN, LEN)]
                partner = gw[:, pl.ds(2 * yo * LEN, LAGS * LEN)]
                prod = lax.dot_general(
                    own, partner, (((0,), (0,)), ((), ())), preferred_element_type=F32
                )
                for lag in range(LAGS):
                    top = prod[:IN_DEV, lag * LEN : (lag + 1) * LEN]
                    low = prod[IN_DEV:, lag * LEN : (lag + 1) * LEN]
                    both = top * sign + pltpu.roll(low, IN_DEV, 1) * scale
                    ob[slot, yo, lag] = both.astype(BF)
            ch = half * RAD + y * KK + kk
            pltpu.make_async_copy(ob.at[slot, y], out_ref.at[ch], o_recv).start()

            @pl.loop(1, NY)
            def _(j):
                to = (y + j) % NY
                pltpu.make_async_remote_copy(
                    src_ref=ob.at[slot, to],
                    dst_ref=out_ref.at[ch],
                    send_sem=o_send,
                    recv_sem=o_recv,
                    device_id={"chan": chan, "stn": to * NZH + zh},
                    device_id_type=MESH,
                ).start()

    pltpu.make_async_copy(out_ref, out_ref, o_recv).wait()
    for slot in range(3):
        pltpu.make_async_copy(halo.at[slot], halo.at[slot], halo_send.at[slot]).wait()
    sent = b1.at[:, pl.ds(0, PLANE - 1)]
    pltpu.make_async_copy(sent, sent, xy_send).wait()
    sent = zr.at[:, pl.ds(0, NZ - 1)]
    pltpu.make_async_copy(sent, sent, z_send).wait()
    sent = ob.at[:, pl.ds(0, NY - 1)]
    pltpu.make_async_copy(sent, sent, o_send).wait()


def local(voltages):
    vmem = pl.BlockSpec(memory_space=pltpu.VMEM)
    dma = pltpu.SemaphoreType.DMA
    products = pl.pallas_call(
        kernel,
        out_shape=jax.ShapeDtypeStruct((2 * RAD, LAGS, IN_DEV, LEN), BF),
        in_specs=[vmem] * 6,
        out_specs=pl.BlockSpec(memory_space=pl.ANY),
        scratch_shapes=[
            pltpu.VMEM((3, 2, IN_DEV, NCH), BF),
            pltpu.VMEM((2, RAD, 2 * IN_DEV, 2 * LEN), BF),
            pltpu.VMEM((2, RAD, 2 * IN_DEV, 2 * LEN), BF),
            pltpu.VMEM((CHUNKS, PLANE, 2, 16, LEN), BF),
            pltpu.VMEM((CHUNKS, PLANE, 2, 16, LEN), BF),
            pltpu.VMEM((CHUNKS, NZL, 2, NY, 16, LEN), BF),
            pltpu.VMEM((CHUNKS, NZ, 2, NY, 16, LEN), BF),
            pltpu.VMEM((256, (STN + LAGS - 1) * LEN), BF),
            pltpu.VMEM((2 * KK, NY, LAGS, IN_DEV, LEN), BF),
            dma((3,)),
            dma((3,)),
            dma,
            dma((CHUNKS,)),
            dma,
            dma((CHUNKS,)),
            dma,
            dma,
        ],
        compiler_params=pltpu.CompilerParams(
            collective_id=0, has_side_effects=True, vmem_limit_bytes=48 * 2**20
        ),
    )(voltages, *(jnp.asarray(t) for t in tables()))
    return jnp.transpose(products, (0, 2, 1, 3))


def solution(mesh):
    return jax.shard_map(
        local,
        mesh=mesh,
        in_specs=(P(None, "stn", "chan"),),
        out_specs=P("chan", "stn", None, None),
        check_vma=False,
    )
```

```python
import math

import jax
import jax.numpy as jnp
import numpy as np
from jax import lax
from jax.experimental import pallas as pl
from jax.experimental.pallas import tpu as pltpu
from jax.sharding import PartitionSpec as P

MESH = pl.DeviceIdType.MESH
NCH = 2048
TAPS = 4
SPEC = 4
RAD = 16
LEN = 128
IN_DEV = 64
NX, NZL, NCORE, NY, NZH = 4, 8, 2, 4, 2
NXC = NX * NCORE
PLANE = NXC * NY
NZ = NZL * NZH
CHAN = NX * NZL * NCORE
STN = NY * NZH
LAGS = STN // 2 + 1
KK = RAD // NY
TURN = TAPS * RAD
CHUNKS = 2 * KK
BF = jnp.bfloat16
F32 = jnp.float32


def tables():
    position = np.arange(TAPS * NCH, dtype=np.float64) + 0.5
    centered = (position - TAPS * NCH / 2.0) / NCH
    window = 0.5 - 0.5 * np.cos(2.0 * math.pi * position / (TAPS * NCH))
    weights = (np.sinc(centered) * window).reshape(TAPS * RAD, LEN).astype(np.float32)
    angle = 2.0 * math.pi / NCH * np.outer(np.arange(RAD), np.arange(LEN))
    twiddle = np.concatenate([np.cos(angle), np.sin(angle)], axis=0).astype(np.float32)
    x, core, zl, half = np.meshgrid(
        np.arange(NX), np.arange(NCORE), np.arange(NZL), np.arange(2), indexing="ij"
    )
    order = (((x * NZL + zl) * NCORE + core) * 2 + half).reshape(-1)
    angle = 2.0 * math.pi / LEN * (np.outer(order, np.arange(LEN)) % LEN)
    table = np.concatenate([np.cos(angle), np.sin(angle)], axis=1) * NCH**-0.5
    high = table.astype(np.float32).astype(BF)
    low = (table - high.astype(np.float64)).astype(np.float32).astype(BF)
    swap = np.zeros((16, 16, 16, 16), np.float32)
    for t in range(16):
        for j in range(16):
            swap[j, t, t, j] = 1.0
    swap = swap.reshape(256, 256).astype(BF)
    return np.concatenate([weights, twiddle]), np.concatenate([high, low, swap])


def transform(points):
    count = len(points)
    if count == 1:
        return points
    even, odd = transform(points[0::2]), transform(points[1::2])
    low, high = [], []
    for k in range(count // 2):
        re, im = odd[k]
        if k == 0:
            pass
        elif 4 * k == count:
            re, im = im, -re
        elif 8 * k == count:
            re, im = (re + im) * math.sqrt(0.5), (im - re) * math.sqrt(0.5)
        elif 8 * k == 3 * count:
            re, im = (im - re) * math.sqrt(0.5), (re + im) * -math.sqrt(0.5)
        else:
            c, s = math.cos(2 * math.pi * k / count), math.sin(2 * math.pi * k / count)
            re, im = re * c + im * s, im * c - re * s
        low.append((even[k][0] + re, even[k][1] + im))
        high.append((even[k][0] - re, even[k][1] - im))
    return low + high


def kernel(
    volt_ref, real_ref, half_ref, out_ref,
    x_ref, real, table, halo, yh, yl, b1, r1, zs, zr, gw, ob,
    load, halo_send, halo_recv, xy_send, xy_recv, z_send, z_recv, o_send, o_recv,
):
    chan, stn = lax.axis_index("chan"), lax.axis_index("stn")
    core = chan % NCORE
    zl = (chan // NCORE) % NZL
    x = chan // (NCORE * NZL)
    y, zh = stn // NZH, stn % NZH
    me_xy = y * NXC + x * NCORE + core
    me_z = zh * NZL + zl

    def at_xy(i):
        xc = i % NXC
        return {"chan": ((xc // NCORE) * NZL + zl) * NCORE + xc % NCORE, "stn": (i // NXC) * NZH + zh}

    def at_z(i):
        return {"chan": (x * NZL + i % NZL) * NCORE + core, "stn": y * NZH + i // NZL}

    after = {"chan": (chan + 1) % CHAN, "stn": stn}
    before = {"chan": (chan + CHAN - 1) % CHAN, "stn": stn}

    loads = [
        pltpu.make_async_copy(src, dst, load.at[i])
        for i, (src, dst) in enumerate(((volt_ref, x_ref), (real_ref, real), (half_ref, table)))
    ]
    for copy in loads:
        copy.start()

    barrier = pltpu.get_barrier_semaphore()

    def greet(device):
        pl.semaphore_signal(barrier, inc=1, device_id=device, device_id_type=MESH)

    greet(after)
    greet(before)

    @pl.loop(1, PLANE)
    def _(j):
        greet(at_xy((me_xy + j) % PLANE))

    @pl.loop(1, NZ)
    def _(j):
        greet(at_z((me_z + j) % NZ))

    pl.semaphore_wait(barrier, PLANE + NZ)

    def send_halo(block, slot):
        pltpu.make_async_remote_copy(
            src_ref=volt_ref.at[:, :, pl.ds(block * NCH, NCH)],
            dst_ref=halo.at[slot],
            send_sem=halo_send.at[slot],
            recv_sem=halo_recv.at[slot],
            device_id=after,
            device_id_type=MESH,
        ).start()

    def wait_halo(slot):
        pltpu.make_async_copy(halo.at[slot], halo.at[slot], halo_recv.at[slot]).wait()

    send_halo(3, 2)
    for copy in loads:
        copy.wait()
    valid = (chan > 0).astype(F32)

    def spectrum(s):
        @pl.loop(0, IN_DEV // 16)
        def _(tile):
            rows = pl.ds(pl.multiple_of(tile * 16, 16), 16)
            points = []
            for a in range(RAD):
                pair = []
                for part in range(2):
                    here = there = None
                    for tap in range(TAPS):
                        w = real[pl.ds(tap * RAD + a, 1), :]
                        j = s - 3 + tap
                        if j >= 0:
                            v = x_ref[part, rows, pl.ds(j * NCH + a * LEN, LEN)].astype(F32) * w
                            here = v if here is None else here + v
                        else:
                            v = halo[3 + j, part, rows, pl.ds(a * LEN, LEN)].astype(F32) * w
                            there = v if there is None else there + v
                    pair.append(here if there is None else here + there * valid)
                points.append(tuple(pair))
            turned = transform(points)
            low_rows = pl.ds(pl.multiple_of(IN_DEV + tile * 16, 16), 16)
            for k in range(RAD):
                re, im = turned[k]
                if k > 0:
                    c, sn = real[pl.ds(TURN + k, 1), :], real[pl.ds(TURN + RAD + k, 1), :]
                    re, im = re * c + im * sn, im * c - re * sn
                re_h, im_h = re.astype(BF), im.astype(BF)
                re_l = (re - re_h.astype(F32)).astype(BF)
                im_l = (im - im_h.astype(F32)).astype(BF)
                for ref, r, i in ((yh, re_h, im_h), (yl, re_l, im_l)):
                    ref[s % 2, k, rows, 0:LEN] = r
                    ref[s % 2, k, rows, LEN : 2 * LEN] = i
                    ref[s % 2, k, low_rows, 0:LEN] = i
                    ref[s % 2, k, low_rows, LEN : 2 * LEN] = -r

    def dot_nt(a, b):
        return lax.dot_general(a, b, (((1,), (1,)), ((), ())), preferred_element_type=F32)

    def channels(chunk, kk):
        @pl.loop(0, NY)
        def _(yd):
            k = yd * KK + kk
            for s in range(2):
                high, low = yh[s, k], yl[s, k]
                o = dot_nt(table[0:LEN], high) + dot_nt(table[LEN : 2 * LEN], high) + dot_nt(table[0:LEN], low)
                b1[chunk, pl.ds(yd * NXC, NXC), s] = o.astype(BF).reshape(NXC, 16, LEN)

        pltpu.make_async_copy(b1.at[chunk, me_xy], r1.at[chunk, me_xy], xy_recv.at[chunk]).start()

        @pl.loop(1, PLANE)
        def _(j):
            to = (me_xy + j) % PLANE
            pltpu.make_async_remote_copy(
                src_ref=b1.at[chunk, to],
                dst_ref=r1.at[chunk, me_xy],
                send_sem=xy_send,
                recv_sem=xy_recv.at[chunk],
                device_id=at_xy(to),
                device_id_type=MESH,
            ).start()

    def spread(chunk, last=False):
        pltpu.make_async_copy(r1.at[chunk], r1.at[chunk], xy_recv.at[chunk]).wait()

        @pl.loop(0, NY)
        def _(yd):
            rows = r1[chunk, pl.ds(yd * NXC, NXC)].reshape(256, LEN)
            o = jnp.dot(table[2 * LEN : 4 * LEN], rows, preferred_element_type=F32).astype(BF)
            zs[chunk, :, :, yd] = o.reshape(NZL, 2, 16, LEN)

        def send(part, sem, to):
            pltpu.make_async_remote_copy(
                src_ref=zs.at[(chunk, to % NZL, *part)],
                dst_ref=zr.at[(chunk, me_z, *part)],
                send_sem=z_send,
                recv_sem=sem,
                device_id=at_z(to),
                device_id_type=MESH,
            ).start()

        if not last:
            sem = z_recv.at[chunk]
            pltpu.make_async_copy(zs.at[chunk, zl], zr.at[chunk, me_z], sem).start()

            @pl.loop(1, NZ)
            def _(j):
                send((), sem, (me_z + NZ // 2 + (j // 2) * (1 - 2 * (j % 2)) + NZ) % NZ)

        else:
            for half in range(2):
                pltpu.make_async_copy(
                    zs.at[chunk, zl, half], zr.at[chunk, me_z, half], z_recv.at[chunk + half]
                ).start()
            for lo, hi in ((0, 4), (4, NZ)):
                for half in range(2):

                    @pl.loop(lo, hi)
                    def _(to, half=half):
                        @pl.when(to != me_z)
                        def _():
                            send((half,), z_recv.at[chunk + half], to)

    def phase(base, last):
        channels(base, 0)

        @pl.loop(1, KK)
        def _(kk):
            channels(base + kk, kk)
            spread(base + kk - 1)

        spread(base + KK - 1, last)

    spectrum(3)
    wait_halo(2)
    send_halo(2, 1)
    send_halo(1, 0)
    spectrum(2)
    phase(0, False)
    wait_halo(1)
    spectrum(1)
    wait_halo(0)
    spectrum(0)
    phase(KK, True)

    lane = lax.broadcasted_iota(jnp.int32, (IN_DEV, LEN), 1)
    scale = 1.0 / (CHAN * SPEC)
    sign = jnp.where(lane < IN_DEV, scale, -scale).astype(F32)

    def correlate(half, kk):
        for g in range(STN + LAGS - 1):
            st = (zh + g) % STN
            for sp in range(2):
                part = zr[sp * KK + kk, pl.ds((st % NZH) * NZL, NZL), half, st // NZH]
                gw[pl.ds(sp * 128, 128), pl.ds(g * LEN, LEN)] = part.reshape(128, LEN)
        slot = half * KK + kk
        for yo in range(NY):
            own = gw[:, pl.ds(2 * yo * LEN, LEN)]
            partner = gw[:, pl.ds(2 * yo * LEN, LAGS * LEN)]
            prod = lax.dot_general(
                own, partner, (((0,), (0,)), ((), ())), preferred_element_type=F32
            )
            for lag in range(LAGS):
                top = prod[:IN_DEV, lag * LEN : (lag + 1) * LEN]
                low = prod[IN_DEV:, lag * LEN : (lag + 1) * LEN]
                both = top * sign + pltpu.roll(low, IN_DEV, 1) * scale
                ob[slot, yo, lag] = both.astype(BF)
        ch = half * RAD + y * KK + kk
        pltpu.make_async_copy(ob.at[slot, y], out_ref.at[ch], o_recv).start()

        @pl.loop(1, NY)
        def _(j):
            to = (y + j) % NY
            pltpu.make_async_remote_copy(
                src_ref=ob.at[slot, to],
                dst_ref=out_ref.at[ch],
                send_sem=o_send,
                recv_sem=o_recv,
                device_id={"chan": chan, "stn": to * NZH + zh},
                device_id_type=MESH,
            ).start()

    def arrived(chunk, *half):
        here = zr.at[(chunk, slice(None), *half)]
        pltpu.make_async_copy(here, here, z_recv.at[chunk + sum(half)]).wait()

    @pl.loop(0, KK - 1)
    def _(kk):
        arrived(kk)
        arrived(KK + kk)

        @pl.loop(0, 2)
        def _(half):
            correlate(half, kk)

    arrived(KK - 1)
    for half in range(2):
        arrived(CHUNKS - 1, half)
        correlate(half, KK - 1)

    pltpu.make_async_copy(out_ref, out_ref, o_recv).wait()
    for slot in range(3):
        pltpu.make_async_copy(halo.at[slot], halo.at[slot], halo_send.at[slot]).wait()
    sent = b1.at[:, pl.ds(0, PLANE - 1)]
    pltpu.make_async_copy(sent, sent, xy_send).wait()
    sent = zr.at[:, pl.ds(0, NZ - 1)]
    pltpu.make_async_copy(sent, sent, z_send).wait()
    sent = ob.at[:, pl.ds(0, NY - 1)]
    pltpu.make_async_copy(sent, sent, o_send).wait()


def local(voltages):
    dma = pltpu.SemaphoreType.DMA
    products = pl.pallas_call(
        kernel,
        out_shape=jax.ShapeDtypeStruct((2 * RAD, LAGS, IN_DEV, LEN), BF),
        in_specs=[pl.BlockSpec(memory_space=pl.ANY)] * 3,
        out_specs=pl.BlockSpec(memory_space=pl.ANY),
        scratch_shapes=[
            pltpu.VMEM((2, IN_DEV, SPEC * NCH), BF),
            pltpu.VMEM((TURN + 2 * RAD, LEN), F32),
            pltpu.VMEM((4 * LEN, 2 * LEN), BF),
            pltpu.VMEM((3, 2, IN_DEV, NCH), BF),
            pltpu.VMEM((2, RAD, 2 * IN_DEV, 2 * LEN), BF),
            pltpu.VMEM((2, RAD, 2 * IN_DEV, 2 * LEN), BF),
            pltpu.VMEM((CHUNKS, PLANE, 2, 16, LEN), BF),
            pltpu.VMEM((CHUNKS, PLANE, 2, 16, LEN), BF),
            pltpu.VMEM((CHUNKS, NZL, 2, NY, 16, LEN), BF),
            pltpu.VMEM((CHUNKS, NZ, 2, NY, 16, LEN), BF),
            pltpu.VMEM((256, (STN + LAGS - 1) * LEN), BF),
            pltpu.VMEM((2 * KK, NY, LAGS, IN_DEV, LEN), BF),
            dma((3,)),
            dma((3,)),
            dma((3,)),
            dma,
            dma((CHUNKS,)),
            dma,
            dma((CHUNKS + 1,)),
            dma,
            dma,
        ],
        compiler_params=pltpu.CompilerParams(
            collective_id=0, has_side_effects=True, vmem_limit_bytes=60 * 2**20
        ),
    )(voltages, *(jnp.asarray(t) for t in tables()))
    return jnp.transpose(products, (0, 2, 1, 3))


def solution(mesh):
    return jax.shard_map(
        local,
        mesh=mesh,
        in_specs=(P(None, "stn", "chan"),),
        out_specs=P("chan", "stn", None, None),
        check_vma=False,
    )
```

```python
import math

import jax
import jax.numpy as jnp
import numpy as np
from jax import lax
from jax.experimental import pallas as pl
from jax.experimental.pallas import tpu as pltpu
from jax.sharding import PartitionSpec as P

MESH = pl.DeviceIdType.MESH
NCH = 2048
TAPS = 4
SPEC = 4
RAD = 16
LEN = 128
IN_DEV = 64
NX, NZL, NCORE, NY, NZH = 4, 8, 2, 4, 2
NXC = NX * NCORE
PLANE = NXC * NY
NZ = NZL * NZH
CHAN = NX * NZL * NCORE
STN = NY * NZH
LAGS = STN // 2 + 1
KK = RAD // NY
TURN = TAPS * RAD
CHUNKS = 2 * KK
BF = jnp.bfloat16
F32 = jnp.float32


def tables():
    position = np.arange(TAPS * NCH, dtype=np.float64) + 0.5
    centered = (position - TAPS * NCH / 2.0) / NCH
    window = 0.5 - 0.5 * np.cos(2.0 * math.pi * position / (TAPS * NCH))
    weights = (np.sinc(centered) * window).reshape(TAPS * RAD, LEN).astype(np.float32)
    angle = 2.0 * math.pi / NCH * np.outer(np.arange(RAD), np.arange(LEN))
    twiddle = np.concatenate([np.cos(angle), np.sin(angle)], axis=0).astype(np.float32)
    x, core, zl, half = np.meshgrid(
        np.arange(NX), np.arange(NCORE), np.arange(NZL), np.arange(2), indexing="ij"
    )
    order = (((x * NZL + zl) * NCORE + core) * 2 + half).reshape(-1)
    angle = 2.0 * math.pi / LEN * (np.outer(order, np.arange(LEN)) % LEN)
    table = np.concatenate([np.cos(angle), np.sin(angle)], axis=1) * NCH**-0.5
    high = table.astype(np.float32).astype(BF)
    low = (table - high.astype(np.float64)).astype(np.float32).astype(BF)
    swap = np.zeros((16, 16, 16, 16), np.float32)
    for t in range(16):
        for j in range(16):
            swap[j, t, t, j] = 1.0
    swap = swap.reshape(256, 256).astype(BF)
    return np.concatenate([weights, twiddle]), np.concatenate([high, low, swap])


def transform(points):
    count = len(points)
    if count == 1:
        return points
    even, odd = transform(points[0::2]), transform(points[1::2])
    low, high = [], []
    for k in range(count // 2):
        re, im = odd[k]
        if k == 0:
            pass
        elif 4 * k == count:
            re, im = im, -re
        elif 8 * k == count:
            re, im = (re + im) * math.sqrt(0.5), (im - re) * math.sqrt(0.5)
        elif 8 * k == 3 * count:
            re, im = (im - re) * math.sqrt(0.5), (re + im) * -math.sqrt(0.5)
        else:
            c, s = math.cos(2 * math.pi * k / count), math.sin(2 * math.pi * k / count)
            re, im = re * c + im * s, im * c - re * s
        low.append((even[k][0] + re, even[k][1] + im))
        high.append((even[k][0] - re, even[k][1] - im))
    return low + high


def kernel(
    volt_ref, real_ref, half_ref, out_ref,
    x_ref, real, table, halo, yh, yl, b1, r1, zs, zr, gw, ob,
    load, halo_send, halo_recv, xy_send, xy_recv, z_send, z_recv, o_send, o_recv,
):
    chan, stn = lax.axis_index("chan"), lax.axis_index("stn")
    core = chan % NCORE
    zl = (chan // NCORE) % NZL
    x = chan // (NCORE * NZL)
    y, zh = stn // NZH, stn % NZH
    me_xy = y * NXC + x * NCORE + core
    me_z = zh * NZL + zl

    def at_xy(i):
        xc = i % NXC
        return {"chan": ((xc // NCORE) * NZL + zl) * NCORE + xc % NCORE, "stn": (i // NXC) * NZH + zh}

    def at_z(i):
        return {"chan": (x * NZL + i % NZL) * NCORE + core, "stn": y * NZH + i // NZL}

    after = {"chan": (chan + 1) % CHAN, "stn": stn}
    before = {"chan": (chan + CHAN - 1) % CHAN, "stn": stn}

    loads = [
        pltpu.make_async_copy(src, dst, load.at[i])
        for i, (src, dst) in enumerate(((volt_ref, x_ref), (real_ref, real), (half_ref, table)))
    ]
    for copy in loads:
        copy.start()

    barrier = pltpu.get_barrier_semaphore()

    def greet(device):
        pl.semaphore_signal(barrier, inc=1, device_id=device, device_id_type=MESH)

    greet(after)
    greet(before)

    @pl.loop(1, NZ)
    def _(j):
        greet(at_z((me_z + j) % NZ))

    @pl.loop(1, PLANE)
    def _(j):
        greet(at_xy((me_xy + j) % PLANE))

    pl.semaphore_wait(barrier, PLANE + NZ)

    def send_halo(block, slot):
        pltpu.make_async_remote_copy(
            src_ref=volt_ref.at[:, :, pl.ds(block * NCH, NCH)],
            dst_ref=halo.at[slot],
            send_sem=halo_send.at[slot],
            recv_sem=halo_recv.at[slot],
            device_id=after,
            device_id_type=MESH,
        ).start()

    def wait_halo(slot):
        pltpu.make_async_copy(halo.at[slot], halo.at[slot], halo_recv.at[slot]).wait()

    send_halo(3, 2)
    for copy in loads:
        copy.wait()
    valid = (chan > 0).astype(F32)

    def spectrum(s):
        @pl.loop(0, IN_DEV // 16)
        def _(tile):
            rows = pl.ds(pl.multiple_of(tile * 16, 16), 16)
            points = []
            for a in range(RAD):
                pair = []
                for part in range(2):
                    here = there = None
                    for tap in range(TAPS):
                        w = real[pl.ds(tap * RAD + a, 1), :]
                        j = s - 3 + tap
                        if j >= 0:
                            v = x_ref[part, rows, pl.ds(j * NCH + a * LEN, LEN)].astype(F32) * w
                            here = v if here is None else here + v
                        else:
                            v = halo[3 + j, part, rows, pl.ds(a * LEN, LEN)].astype(F32) * w
                            there = v if there is None else there + v
                    pair.append(here if there is None else here + there * valid)
                points.append(tuple(pair))
            turned = transform(points)
            low_rows = pl.ds(pl.multiple_of(IN_DEV + tile * 16, 16), 16)
            for k in range(RAD):
                re, im = turned[k]
                if k > 0:
                    c, sn = real[pl.ds(TURN + k, 1), :], real[pl.ds(TURN + RAD + k, 1), :]
                    re, im = re * c + im * sn, im * c - re * sn
                re_h, im_h = re.astype(BF), im.astype(BF)
                re_l = (re - re_h.astype(F32)).astype(BF)
                im_l = (im - im_h.astype(F32)).astype(BF)
                for ref, r, i in ((yh, re_h, im_h), (yl, re_l, im_l)):
                    ref[s % 2, k, rows, 0:LEN] = r
                    ref[s % 2, k, rows, LEN : 2 * LEN] = i
                    ref[s % 2, k, low_rows, 0:LEN] = i
                    ref[s % 2, k, low_rows, LEN : 2 * LEN] = -r

    def dot_nt(a, b):
        return lax.dot_general(a, b, (((1,), (1,)), ((), ())), preferred_element_type=F32)

    def channels(chunk):
        @pl.loop(0, NY)
        def _(yd):
            k = yd * KK + chunk % KK
            for s in range(2):
                high, low = yh[s, k], yl[s, k]
                o = dot_nt(table[0:LEN], high) + dot_nt(table[LEN : 2 * LEN], high) + dot_nt(table[0:LEN], low)
                b1[chunk, pl.ds(yd * NXC, NXC), s] = o.astype(BF).reshape(NXC, 16, LEN)

    def trade(first, count, sem):
        some = pl.ds(first, count)
        pltpu.make_async_copy(b1.at[some, me_xy], r1.at[some, me_xy], sem).start()

        @pl.loop(1, PLANE)
        def _(j):
            to = (me_xy + j) % PLANE
            pltpu.make_async_remote_copy(
                src_ref=b1.at[some, to],
                dst_ref=r1.at[some, me_xy],
                send_sem=xy_send,
                recv_sem=sem,
                device_id=at_xy(to),
                device_id_type=MESH,
            ).start()

    def traded(first, count, sem):
        here = r1.at[pl.ds(first, count)]
        pltpu.make_async_copy(here, here, sem).wait()

    def spread(chunk):
        @pl.loop(0, NY)
        def _(yd):
            rows = r1[chunk, pl.ds(yd * NXC, NXC)].reshape(256, LEN)
            o = jnp.dot(table[2 * LEN : 4 * LEN], rows, preferred_element_type=F32).astype(BF)
            zs[chunk, :, :, yd] = o.reshape(NZL, 2, 16, LEN)

    def send(chunks, part, sem, to):
        pltpu.make_async_remote_copy(
            src_ref=zs.at[(chunks, to % NZL, *part)],
            dst_ref=zr.at[(chunks, me_z, *part)],
            send_sem=z_send,
            recv_sem=sem,
            device_id=at_z(to),
            device_id_type=MESH,
        ).start()

    def pass_on(first, count, sem):
        some = pl.ds(first, count)
        pltpu.make_async_copy(zs.at[some, zl], zr.at[some, me_z], sem).start()

        @pl.loop(1, NZ)
        def _(j):
            send(some, (), sem, (me_z + NZ // 2 + (j // 2) * (1 - 2 * (j % 2)) * (1 - 2 * core) + NZ) % NZ)

    def pass_last(chunk, sems):
        for half in range(2):
            pltpu.make_async_copy(zs.at[chunk, zl, half], zr.at[chunk, me_z, half], sems[half]).start()
        for lo, hi in ((0, 4), (4, NZ)):
            for half in range(2):

                @pl.loop(lo, hi)
                def _(to, half=half):
                    @pl.when(to != me_z)
                    def _():
                        send(chunk, (half,), sems[half], to)

    def arrived(sem, chunks, *half):
        here = zr.at[(chunks, slice(None), *half)]
        pltpu.make_async_copy(here, here, sem).wait()

    def some(first, count, step):
        pl.loop(first, first + count)(step)

    spectrum(3)
    wait_halo(2)
    send_halo(2, 1)
    send_halo(1, 0)
    spectrum(2)
    channels(0)
    trade(0, 1, xy_recv.at[0])
    some(1, KK - 1, channels)
    trade(1, KK - 1, xy_recv.at[1])
    traded(0, 1, xy_recv.at[0])
    spread(0)
    pass_on(0, 1, z_recv.at[0])
    traded(1, KK - 1, xy_recv.at[1])
    some(1, KK - 1, spread)
    pass_on(1, KK - 1, z_recv.at[1])
    wait_halo(1)
    spectrum(1)
    wait_halo(0)
    spectrum(0)
    some(KK, KK, channels)
    trade(KK, KK, xy_recv.at[2])
    traded(KK, KK, xy_recv.at[2])
    some(KK, KK, spread)
    pass_on(KK, 2, z_recv.at[2])
    pass_on(KK + 2, 1, z_recv.at[3])
    pass_last(CHUNKS - 1, (z_recv.at[4], z_recv.at[5]))

    lane = lax.broadcasted_iota(jnp.int32, (IN_DEV, LEN), 1)
    scale = 1.0 / (CHAN * SPEC)
    sign = jnp.where(lane < IN_DEV, scale, -scale).astype(F32)

    def correlate(half, kk):
        for g in range(STN + LAGS - 1):
            st = (zh + g) % STN
            for sp in range(2):
                part = zr[sp * KK + kk, pl.ds((st % NZH) * NZL, NZL), half, st // NZH]
                gw[pl.ds(sp * 128, 128), pl.ds(g * LEN, LEN)] = part.reshape(128, LEN)
        slot = half * KK + kk
        ch = half * RAD + y * KK + kk

        def products(to):
            at = pl.multiple_of(2 * to * LEN, LEN)
            prod = lax.dot_general(
                gw[:, pl.ds(at, LEN)],
                gw[:, pl.ds(at, LAGS * LEN)],
                (((0,), (0,)), ((), ())),
                preferred_element_type=F32,
            )
            for lag in range(LAGS):
                top = prod[:IN_DEV, lag * LEN : (lag + 1) * LEN]
                low = prod[IN_DEV:, lag * LEN : (lag + 1) * LEN]
                whole = top * sign + pltpu.roll(low, IN_DEV, 1) * scale
                ob[slot, to, lag] = whole.astype(BF)

        @pl.loop(0, NY - 1)
        def _(j):
            to = (y + (j + 1) % (NY - 1) + 1) % NY
            products(to)
            pltpu.make_async_remote_copy(
                src_ref=ob.at[slot, to],
                dst_ref=out_ref.at[ch],
                send_sem=o_send,
                recv_sem=o_recv,
                device_id={"chan": chan, "stn": to * NZH + zh},
                device_id_type=MESH,
            ).start()

        products(y)
        pltpu.make_async_copy(ob.at[slot, y], out_ref.at[ch], o_recv).start()

    def both(kk):
        pl.loop(0, 2)(lambda half: correlate(half, kk))

    arrived(z_recv.at[0], 0)
    arrived(z_recv.at[1], pl.ds(1, KK - 1))
    arrived(z_recv.at[2], pl.ds(KK, 2))
    some(0, 2, both)
    arrived(z_recv.at[3], KK + 2)
    both(2)
    for half in range(2):
        arrived(z_recv.at[4 + half], CHUNKS - 1, half)
        correlate(half, KK - 1)

    pltpu.make_async_copy(out_ref, out_ref, o_recv).wait()
    for slot in range(3):
        pltpu.make_async_copy(halo.at[slot], halo.at[slot], halo_send.at[slot]).wait()
    sent = b1.at[:, pl.ds(0, PLANE - 1)]
    pltpu.make_async_copy(sent, sent, xy_send).wait()
    sent = zr.at[:, pl.ds(0, NZ - 1)]
    pltpu.make_async_copy(sent, sent, z_send).wait()
    sent = ob.at[:, pl.ds(0, NY - 1)]
    pltpu.make_async_copy(sent, sent, o_send).wait()


def finish(src, dst, held, sems, more):
    parts = [pl.ds(8 * i, 8) for i in range(4)]
    for i, part in enumerate(parts):
        pltpu.make_async_copy(src.at[part], held.at[part], sems.at[i]).start()
    for i, part in enumerate(parts):
        pltpu.make_async_copy(src.at[part], held.at[part], sems.at[i]).wait()
        pltpu.make_async_copy(held.at[part], dst.at[part], more.at[i]).start()
    for i, part in enumerate(parts):
        pltpu.make_async_copy(held.at[part], dst.at[part], more.at[i]).wait()


def local(voltages):
    dma = pltpu.SemaphoreType.DMA
    products = pl.pallas_call(
        kernel,
        out_shape=jax.ShapeDtypeStruct((2 * RAD, LAGS, IN_DEV, LEN), BF),
        in_specs=[pl.BlockSpec(memory_space=pl.ANY)] * 3,
        out_specs=pl.BlockSpec(memory_space=pl.ANY),
        scratch_shapes=[
            pltpu.VMEM((2, IN_DEV, SPEC * NCH), BF),
            pltpu.VMEM((TURN + 2 * RAD, LEN), F32),
            pltpu.VMEM((4 * LEN, 2 * LEN), BF),
            pltpu.VMEM((3, 2, IN_DEV, NCH), BF),
            pltpu.VMEM((2, RAD, 2 * IN_DEV, 2 * LEN), BF),
            pltpu.VMEM((2, RAD, 2 * IN_DEV, 2 * LEN), BF),
            pltpu.VMEM((CHUNKS, PLANE, 2, 16, LEN), BF),
            pltpu.VMEM((CHUNKS, PLANE, 2, 16, LEN), BF),
            pltpu.VMEM((CHUNKS, NZL, 2, NY, 16, LEN), BF),
            pltpu.VMEM((CHUNKS, NZ, 2, NY, 16, LEN), BF),
            pltpu.VMEM((256, (STN + LAGS - 1) * LEN), BF),
            pltpu.VMEM((2 * KK, NY, LAGS, IN_DEV, LEN), BF),
            dma((3,)),
            dma((3,)),
            dma((3,)),
            dma,
            dma((3,)),
            dma,
            dma((6,)),
            dma,
            dma,
        ],
        compiler_params=pltpu.CompilerParams(
            collective_id=0, has_side_effects=True, vmem_limit_bytes=60 * 2**20
        ),
    )(voltages, *(jnp.asarray(t) for t in tables()))
    products = pl.pallas_call(
        finish,
        out_shape=jax.ShapeDtypeStruct((2 * RAD, LAGS, IN_DEV, LEN), BF),
        in_specs=[pl.BlockSpec(memory_space=pl.ANY)],
        out_specs=pl.BlockSpec(memory_space=pl.ANY),
        scratch_shapes=[pltpu.VMEM((2 * RAD, LAGS, IN_DEV, LEN), BF), dma((4,)), dma((4,))],
        compiler_params=pltpu.CompilerParams(vmem_limit_bytes=60 * 2**20),
    )(products)
    return jnp.transpose(products, (0, 2, 1, 3))


def solution(mesh):
    return jax.shard_map(
        local,
        mesh=mesh,
        in_specs=(P(None, "stn", "chan"),),
        out_specs=P("chan", "stn", None, None),
        check_vma=False,
    )
```

```python
import math

import jax
import jax.numpy as jnp
import numpy as np
from jax import lax
from jax.experimental import pallas as pl
from jax.experimental.pallas import tpu as pltpu
from jax.sharding import PartitionSpec as P

MESH = pl.DeviceIdType.MESH
NCH = 2048
TAPS = 4
SPEC = 4
RAD = 16
LEN = 128
IN_DEV = 64
NX, NZL, NCORE, NY, NZH = 4, 8, 2, 4, 2
NXC = NX * NCORE
PLANE = NXC * NY
NZ = NZL * NZH
CHAN = NX * NZL * NCORE
STN = NY * NZH
LAGS = STN // 2 + 1
KK = RAD // NY
TURN = TAPS * RAD
CHUNKS = 2 * KK
BF = jnp.bfloat16
F32 = jnp.float32


def tables():
    position = np.arange(TAPS * NCH, dtype=np.float64) + 0.5
    centered = (position - TAPS * NCH / 2.0) / NCH
    window = 0.5 - 0.5 * np.cos(2.0 * math.pi * position / (TAPS * NCH))
    weights = (np.sinc(centered) * window).reshape(TAPS * RAD, LEN).astype(np.float32)
    angle = 2.0 * math.pi / NCH * np.outer(np.arange(RAD), np.arange(LEN))
    twiddle = np.concatenate([np.cos(angle), np.sin(angle)], axis=0).astype(np.float32)
    x, core, zl, half = np.meshgrid(
        np.arange(NX), np.arange(NCORE), np.arange(NZL), np.arange(2), indexing="ij"
    )
    order = (((x * NZL + zl) * NCORE + core) * 2 + half).reshape(-1)
    angle = 2.0 * math.pi / LEN * (np.outer(order, np.arange(LEN)) % LEN)
    table = np.concatenate([np.cos(angle), np.sin(angle)], axis=1) * NCH**-0.5
    high = table.astype(np.float32).astype(BF)
    low = (table - high.astype(np.float64)).astype(np.float32).astype(BF)
    swap = np.zeros((16, 16, 16, 16), np.float32)
    for t in range(16):
        for j in range(16):
            swap[j, t, t, j] = 1.0
    swap = swap.reshape(256, 256).astype(BF)
    return np.concatenate([weights, twiddle]), np.concatenate([high, low, swap])


def transform(points):
    count = len(points)
    if count == 1:
        return points
    even, odd = transform(points[0::2]), transform(points[1::2])
    low, high = [], []
    for k in range(count // 2):
        re, im = odd[k]
        if k == 0:
            pass
        elif 4 * k == count:
            re, im = im, -re
        elif 8 * k == count:
            re, im = (re + im) * math.sqrt(0.5), (im - re) * math.sqrt(0.5)
        elif 8 * k == 3 * count:
            re, im = (im - re) * math.sqrt(0.5), (re + im) * -math.sqrt(0.5)
        else:
            c, s = math.cos(2 * math.pi * k / count), math.sin(2 * math.pi * k / count)
            re, im = re * c + im * s, im * c - re * s
        low.append((even[k][0] + re, even[k][1] + im))
        high.append((even[k][0] - re, even[k][1] - im))
    return low + high


def kernel(
    volt_ref, real_ref, half_ref, out_ref,
    x_ref, real, table, halo, yh, yl, b1, r1, zs, zr, gw, ob,
    load, halo_send, halo_recv, xy_send, xy_recv, z_send, z_recv, o_send, o_recv,
):
    chan, stn = lax.axis_index("chan"), lax.axis_index("stn")
    core = chan % NCORE
    zl = (chan // NCORE) % NZL
    x = chan // (NCORE * NZL)
    y, zh = stn // NZH, stn % NZH
    me_xy = y * NXC + x * NCORE + core
    me_z = zh * NZL + zl

    def at_xy(i):
        xc = i % NXC
        return {"chan": ((xc // NCORE) * NZL + zl) * NCORE + xc % NCORE, "stn": (i // NXC) * NZH + zh}

    def at_z(i):
        return {"chan": (x * NZL + i % NZL) * NCORE + core, "stn": y * NZH + i // NZL}

    after = {"chan": (chan + 1) % CHAN, "stn": stn}
    before = {"chan": (chan + CHAN - 1) % CHAN, "stn": stn}

    loads = [
        pltpu.make_async_copy(src, dst, load.at[i])
        for i, (src, dst) in enumerate(((volt_ref, x_ref), (real_ref, real), (half_ref, table)))
    ]
    for copy in loads:
        copy.start()

    barrier = pltpu.get_barrier_semaphore()

    def greet(device):
        pl.semaphore_signal(barrier, inc=1, device_id=device, device_id_type=MESH)

    greet(after)
    greet(before)

    @pl.loop(1, NZ)
    def _(j):
        greet(at_z((me_z + j) % NZ))

    @pl.loop(1, PLANE)
    def _(j):
        greet(at_xy((me_xy + j) % PLANE))

    pl.semaphore_wait(barrier, PLANE + NZ)

    def send_halo(block, slot):
        pltpu.make_async_remote_copy(
            src_ref=volt_ref.at[:, :, pl.ds(block * NCH, NCH)],
            dst_ref=halo.at[slot],
            send_sem=halo_send.at[slot],
            recv_sem=halo_recv.at[slot],
            device_id=after,
            device_id_type=MESH,
        ).start()

    def wait_halo(slot):
        pltpu.make_async_copy(halo.at[slot], halo.at[slot], halo_recv.at[slot]).wait()

    send_halo(3, 2)
    for copy in loads:
        copy.wait()
    valid = (chan > 0).astype(F32)

    def spectrum(s):
        @pl.loop(0, IN_DEV // 16)
        def _(tile):
            rows = pl.ds(pl.multiple_of(tile * 16, 16), 16)
            points = []
            for a in range(RAD):
                pair = []
                for part in range(2):
                    here = there = None
                    for tap in range(TAPS):
                        w = real[pl.ds(tap * RAD + a, 1), :]
                        j = s - 3 + tap
                        if j >= 0:
                            v = x_ref[part, rows, pl.ds(j * NCH + a * LEN, LEN)].astype(F32) * w
                            here = v if here is None else here + v
                        else:
                            v = halo[3 + j, part, rows, pl.ds(a * LEN, LEN)].astype(F32) * w
                            there = v if there is None else there + v
                    pair.append(here if there is None else here + there * valid)
                points.append(tuple(pair))
            turned = transform(points)
            low_rows = pl.ds(pl.multiple_of(IN_DEV + tile * 16, 16), 16)
            for k in range(RAD):
                re, im = turned[k]
                if k > 0:
                    c, sn = real[pl.ds(TURN + k, 1), :], real[pl.ds(TURN + RAD + k, 1), :]
                    re, im = re * c + im * sn, im * c - re * sn
                re_h, im_h = re.astype(BF), im.astype(BF)
                re_l = (re - re_h.astype(F32)).astype(BF)
                im_l = (im - im_h.astype(F32)).astype(BF)
                for ref, r, i in ((yh, re_h, im_h), (yl, re_l, im_l)):
                    ref[s % 2, k, rows, 0:LEN] = r
                    ref[s % 2, k, rows, LEN : 2 * LEN] = i
                    ref[s % 2, k, low_rows, 0:LEN] = i
                    ref[s % 2, k, low_rows, LEN : 2 * LEN] = -r

    def dot_nt(a, b):
        return lax.dot_general(a, b, (((1,), (1,)), ((), ())), preferred_element_type=F32)

    def channels(chunk, *parts):
        @pl.loop(0, NY)
        def _(yd):
            k = yd * KK + chunk % KK
            for s in parts:
                high, low = yh[s, k], yl[s, k]
                o = dot_nt(table[0:LEN], high) + dot_nt(table[LEN : 2 * LEN], high) + dot_nt(table[0:LEN], low)
                b1[chunk, pl.ds(yd * NXC, NXC), s] = o.astype(BF).reshape(NXC, 16, LEN)

    def trade(first, count, sem):
        some = pl.ds(first, count)
        pltpu.make_async_copy(b1.at[some, me_xy], r1.at[some, me_xy], sem).start()

        @pl.loop(1, PLANE)
        def _(j):
            to = (me_xy + j) % PLANE
            pltpu.make_async_remote_copy(
                src_ref=b1.at[some, to],
                dst_ref=r1.at[some, me_xy],
                send_sem=xy_send,
                recv_sem=sem,
                device_id=at_xy(to),
                device_id_type=MESH,
            ).start()

    def traded(first, count, sem):
        here = r1.at[pl.ds(first, count)]
        pltpu.make_async_copy(here, here, sem).wait()

    def spread(chunk):
        @pl.loop(0, NY)
        def _(yd):
            rows = r1[chunk, pl.ds(yd * NXC, NXC)].reshape(256, LEN)
            o = jnp.dot(table[2 * LEN : 4 * LEN], rows, preferred_element_type=F32).astype(BF)
            zs[chunk, :, :, yd] = o.reshape(NZL, 2, 16, LEN)

    def send(chunks, part, sem, to):
        pltpu.make_async_remote_copy(
            src_ref=zs.at[(chunks, to % NZL, *part)],
            dst_ref=zr.at[(chunks, me_z, *part)],
            send_sem=z_send,
            recv_sem=sem,
            device_id=at_z(to),
            device_id_type=MESH,
        ).start()

    def pass_on(first, count, sem):
        some = pl.ds(first, count)
        pltpu.make_async_copy(zs.at[some, zl], zr.at[some, me_z], sem).start()

        @pl.loop(1, NZ)
        def _(j):
            send(some, (), sem, (me_z + NZ // 2 + (j // 2) * (1 - 2 * (j % 2)) * (1 - 2 * core) + NZ) % NZ)

    def pass_last(chunk, sems):
        for half in range(2):
            pltpu.make_async_copy(zs.at[chunk, zl, half], zr.at[chunk, me_z, half], sems[half]).start()
        for lo, hi in ((0, 4), (4, NZ)):
            for half in range(2):

                @pl.loop(lo, hi)
                def _(j, lo=lo, hi=hi, half=half):
                    to = j + core * (hi + lo - 1 - 2 * j)

                    @pl.when(to != me_z)
                    def _():
                        send(chunk, (half,), sems[half], to)

    def arrived(sem, chunks, *half):
        here = zr.at[(chunks, slice(None), *half)]
        pltpu.make_async_copy(here, here, sem).wait()

    def some(first, count, step):
        pl.loop(first, first + count)(step)

    spectrum(3)
    some(0, KK, lambda chunk: channels(chunk, 1))
    wait_halo(2)
    send_halo(2, 1)
    send_halo(1, 0)
    spectrum(2)
    channels(0, 0)
    trade(0, 1, xy_recv.at[0])
    traded(0, 1, xy_recv.at[0])
    spread(0)
    pass_on(0, 1, z_recv.at[0])
    some(1, KK - 1, lambda chunk: channels(chunk, 0))
    trade(1, KK - 1, xy_recv.at[1])
    traded(1, KK - 1, xy_recv.at[1])
    some(1, KK - 1, spread)
    pass_on(1, KK - 1, z_recv.at[1])
    wait_halo(1)
    spectrum(1)
    wait_halo(0)
    spectrum(0)
    some(KK, KK, lambda chunk: channels(chunk, 0, 1))
    trade(KK, KK, xy_recv.at[2])
    traded(KK, KK, xy_recv.at[2])
    some(KK, KK, spread)
    pass_on(KK, 2, z_recv.at[2])
    pass_on(KK + 2, 1, z_recv.at[3])
    pass_last(CHUNKS - 1, (z_recv.at[4], z_recv.at[5]))

    lane = lax.broadcasted_iota(jnp.int32, (IN_DEV, LEN), 1)
    scale = 1.0 / (CHAN * SPEC)
    sign = jnp.where(lane < IN_DEV, scale, -scale).astype(F32)

    def correlate(half, kk):
        for g in range(STN + LAGS - 1):
            st = (zh + g) % STN
            for sp in range(2):
                part = zr[sp * KK + kk, pl.ds((st % NZH) * NZL, NZL), half, st // NZH]
                gw[pl.ds(sp * 128, 128), pl.ds(g * LEN, LEN)] = part.reshape(128, LEN)
        slot = half * KK + kk
        ch = half * RAD + y * KK + kk

        def products(to):
            at = pl.multiple_of(2 * to * LEN, LEN)
            prod = lax.dot_general(
                gw[:, pl.ds(at, LEN)],
                gw[:, pl.ds(at, LAGS * LEN)],
                (((0,), (0,)), ((), ())),
                preferred_element_type=F32,
            )
            for lag in range(LAGS):
                top = prod[:IN_DEV, lag * LEN : (lag + 1) * LEN]
                low = prod[IN_DEV:, lag * LEN : (lag + 1) * LEN]
                whole = top * sign + pltpu.roll(low, IN_DEV, 1) * scale
                ob[slot, to, lag] = whole.astype(BF)

        @pl.loop(0, NY - 1)
        def _(j):
            to = (y + (j + 1) % (NY - 1) + 1) % NY
            products(to)
            pltpu.make_async_remote_copy(
                src_ref=ob.at[slot, to],
                dst_ref=out_ref.at[ch],
                send_sem=o_send,
                recv_sem=o_recv,
                device_id={"chan": chan, "stn": to * NZH + zh},
                device_id_type=MESH,
            ).start()

        products(y)
        pltpu.make_async_copy(ob.at[slot, y], out_ref.at[ch], o_recv).start()

    def both(kk):
        pl.loop(0, 2)(lambda half: correlate(half, kk))

    arrived(z_recv.at[0], 0)
    arrived(z_recv.at[1], pl.ds(1, KK - 1))
    arrived(z_recv.at[2], pl.ds(KK, 2))
    some(0, 2, both)
    arrived(z_recv.at[3], KK + 2)
    both(2)
    for half in range(2):
        arrived(z_recv.at[4 + half], CHUNKS - 1, half)
        correlate(half, KK - 1)

    pltpu.make_async_copy(out_ref, out_ref, o_recv).wait()
    for slot in range(3):
        pltpu.make_async_copy(halo.at[slot], halo.at[slot], halo_send.at[slot]).wait()
    sent = b1.at[:, pl.ds(0, PLANE - 1)]
    pltpu.make_async_copy(sent, sent, xy_send).wait()
    sent = zr.at[:, pl.ds(0, NZ - 1)]
    pltpu.make_async_copy(sent, sent, z_send).wait()
    sent = ob.at[:, pl.ds(0, NY - 1)]
    pltpu.make_async_copy(sent, sent, o_send).wait()


def finish(src, dst, held, sems, more):
    parts = [pl.ds(8 * i, 8) for i in range(4)]
    for i, part in enumerate(parts):
        pltpu.make_async_copy(src.at[part], held.at[part], sems.at[i]).start()
    for i, part in enumerate(parts):
        pltpu.make_async_copy(src.at[part], held.at[part], sems.at[i]).wait()
        pltpu.make_async_copy(held.at[part], dst.at[part], more.at[i]).start()
    for i, part in enumerate(parts):
        pltpu.make_async_copy(held.at[part], dst.at[part], more.at[i]).wait()


def local(voltages):
    dma = pltpu.SemaphoreType.DMA
    products = pl.pallas_call(
        kernel,
        out_shape=jax.ShapeDtypeStruct((2 * RAD, LAGS, IN_DEV, LEN), BF),
        in_specs=[pl.BlockSpec(memory_space=pl.ANY)] * 3,
        out_specs=pl.BlockSpec(memory_space=pl.ANY),
        scratch_shapes=[
            pltpu.VMEM((2, IN_DEV, SPEC * NCH), BF),
            pltpu.VMEM((TURN + 2 * RAD, LEN), F32),
            pltpu.VMEM((4 * LEN, 2 * LEN), BF),
            pltpu.VMEM((3, 2, IN_DEV, NCH), BF),
            pltpu.VMEM((2, RAD, 2 * IN_DEV, 2 * LEN), BF),
            pltpu.VMEM((2, RAD, 2 * IN_DEV, 2 * LEN), BF),
            pltpu.VMEM((CHUNKS, PLANE, 2, 16, LEN), BF),
            pltpu.VMEM((CHUNKS, PLANE, 2, 16, LEN), BF),
            pltpu.VMEM((CHUNKS, NZL, 2, NY, 16, LEN), BF),
            pltpu.VMEM((CHUNKS, NZ, 2, NY, 16, LEN), BF),
            pltpu.VMEM((256, (STN + LAGS - 1) * LEN), BF),
            pltpu.VMEM((2 * KK, NY, LAGS, IN_DEV, LEN), BF),
            dma((3,)),
            dma((3,)),
            dma((3,)),
            dma,
            dma((3,)),
            dma,
            dma((6,)),
            dma,
            dma,
        ],
        compiler_params=pltpu.CompilerParams(
            collective_id=0, has_side_effects=True, vmem_limit_bytes=60 * 2**20
        ),
    )(voltages, *(jnp.asarray(t) for t in tables()))
    products = pl.pallas_call(
        finish,
        out_shape=jax.ShapeDtypeStruct((2 * RAD, LAGS, IN_DEV, LEN), BF),
        in_specs=[pl.BlockSpec(memory_space=pl.ANY)],
        out_specs=pl.BlockSpec(memory_space=pl.ANY),
        scratch_shapes=[pltpu.VMEM((2 * RAD, LAGS, IN_DEV, LEN), BF), dma((4,)), dma((4,))],
        compiler_params=pltpu.CompilerParams(vmem_limit_bytes=60 * 2**20),
    )(products)
    return jnp.transpose(products, (0, 2, 1, 3))


def solution(mesh):
    return jax.shard_map(
        local,
        mesh=mesh,
        in_specs=(P(None, "stn", "chan"),),
        out_specs=P("chan", "stn", None, None),
        check_vma=False,
    )
```

```python
import math

import jax
import jax.numpy as jnp
import numpy as np
from jax import lax
from jax.experimental import pallas as pl
from jax.experimental.pallas import tpu as pltpu
from jax.sharding import PartitionSpec as P

MESH = pl.DeviceIdType.MESH
NCH = 2048
TAPS = 4
SPEC = 4
RAD = 16
LEN = 128
IN_DEV = 64
NX, NZL, NCORE, NY, NZH = 4, 8, 2, 4, 2
NXC = NX * NCORE
PLANE = NXC * NY
NZ = NZL * NZH
CHAN = NX * NZL * NCORE
STN = NY * NZH
LAGS = STN // 2 + 1
KK = RAD // NY
TURN = TAPS * RAD
CHUNKS = 2 * KK
BF = jnp.bfloat16
F32 = jnp.float32


def tables():
    position = np.arange(TAPS * NCH, dtype=np.float64) + 0.5
    centered = (position - TAPS * NCH / 2.0) / NCH
    window = 0.5 - 0.5 * np.cos(2.0 * math.pi * position / (TAPS * NCH))
    weights = (np.sinc(centered) * window).reshape(TAPS * RAD, LEN).astype(np.float32)
    angle = 2.0 * math.pi / NCH * np.outer(np.arange(RAD), np.arange(LEN))
    twiddle = np.concatenate([np.cos(angle), np.sin(angle)], axis=0).astype(np.float32)
    x, core, zl, half = np.meshgrid(
        np.arange(NX), np.arange(NCORE), np.arange(NZL), np.arange(2), indexing="ij"
    )
    order = (((x * NZL + zl) * NCORE + core) * 2 + half).reshape(-1)
    angle = 2.0 * math.pi / LEN * (np.outer(order, np.arange(LEN)) % LEN)
    table = np.concatenate([np.cos(angle), np.sin(angle)], axis=1) * NCH**-0.5
    high = table.astype(np.float32).astype(BF)
    low = (table - high.astype(np.float64)).astype(np.float32).astype(BF)
    swap = np.zeros((16, 16, 16, 16), np.float32)
    for t in range(16):
        for j in range(16):
            swap[j, t, t, j] = 1.0
    swap = swap.reshape(256, 256).astype(BF)
    return np.concatenate([weights, twiddle]), np.concatenate([high, low, swap])


def transform(points):
    count = len(points)
    if count == 1:
        return points
    even, odd = transform(points[0::2]), transform(points[1::2])
    low, high = [], []
    for k in range(count // 2):
        re, im = odd[k]
        if k == 0:
            pass
        elif 4 * k == count:
            re, im = im, -re
        elif 8 * k == count:
            re, im = (re + im) * math.sqrt(0.5), (im - re) * math.sqrt(0.5)
        elif 8 * k == 3 * count:
            re, im = (im - re) * math.sqrt(0.5), (re + im) * -math.sqrt(0.5)
        else:
            c, s = math.cos(2 * math.pi * k / count), math.sin(2 * math.pi * k / count)
            re, im = re * c + im * s, im * c - re * s
        low.append((even[k][0] + re, even[k][1] + im))
        high.append((even[k][0] - re, even[k][1] - im))
    return low + high


def kernel(
    volt_ref, real_ref, half_ref, out_ref,
    x_ref, real, table, halo, yh, yl, b1, r1, zs, zr, gw, ob,
    load, halo_send, halo_recv, xy_send, xy_recv, z_send, z_recv, o_send, o_recv,
):
    chan, stn = lax.axis_index("chan"), lax.axis_index("stn")
    core = chan % NCORE
    zl = (chan // NCORE) % NZL
    x = chan // (NCORE * NZL)
    y, zh = stn // NZH, stn % NZH
    me_xy = y * NXC + x * NCORE + core
    me_z = zh * NZL + zl

    def at_xy(i):
        xc = i % NXC
        return {"chan": ((xc // NCORE) * NZL + zl) * NCORE + xc % NCORE, "stn": (i // NXC) * NZH + zh}

    def at_z(i):
        return {"chan": (x * NZL + i % NZL) * NCORE + core, "stn": y * NZH + i // NZL}

    after = {"chan": (chan + 1) % CHAN, "stn": stn}
    before = {"chan": (chan + CHAN - 1) % CHAN, "stn": stn}

    loads = [
        pltpu.make_async_copy(src, dst, load.at[i])
        for i, (src, dst) in enumerate(((volt_ref, x_ref), (real_ref, real), (half_ref, table)))
    ]
    for copy in loads:
        copy.start()

    barrier = pltpu.get_barrier_semaphore()

    def greet(device):
        pl.semaphore_signal(barrier, inc=1, device_id=device, device_id_type=MESH)

    greet(after)
    greet(before)

    @pl.loop(1, NZ)
    def _(j):
        greet(at_z((me_z + j) % NZ))

    @pl.loop(1, PLANE)
    def _(j):
        greet(at_xy((me_xy + j) % PLANE))

    pl.semaphore_wait(barrier, PLANE + NZ)

    def send_halo(block, slot):
        @pl.when(chan < CHAN - 1)
        def _():
            pltpu.make_async_remote_copy(
                src_ref=volt_ref.at[:, :, pl.ds(block * NCH, NCH)],
                dst_ref=halo.at[slot],
                send_sem=halo_send.at[slot],
                recv_sem=halo_recv.at[slot],
                device_id=after,
                device_id_type=MESH,
            ).start()

    def wait_halo(slot):
        @pl.when(chan > 0)
        def _():
            pltpu.make_async_copy(halo.at[slot], halo.at[slot], halo_recv.at[slot]).wait()

    send_halo(3, 2)

    @pl.when(chan == 0)
    def _():
        halo[...] = jnp.zeros_like(halo)

    for copy in loads:
        copy.wait()
    valid = (chan > 0).astype(F32)

    def spectrum(s):
        @pl.loop(0, IN_DEV // 16)
        def _(tile):
            rows = pl.ds(pl.multiple_of(tile * 16, 16), 16)
            points = []
            for a in range(RAD):
                pair = []
                for part in range(2):
                    here = there = None
                    for tap in range(TAPS):
                        w = real[pl.ds(tap * RAD + a, 1), :]
                        j = s - 3 + tap
                        if j >= 0:
                            v = x_ref[part, rows, pl.ds(j * NCH + a * LEN, LEN)].astype(F32) * w
                            here = v if here is None else here + v
                        else:
                            v = halo[3 + j, part, rows, pl.ds(a * LEN, LEN)].astype(F32) * w
                            there = v if there is None else there + v
                    pair.append(here if there is None else here + there * valid)
                points.append(tuple(pair))
            turned = transform(points)
            low_rows = pl.ds(pl.multiple_of(IN_DEV + tile * 16, 16), 16)
            for k in range(RAD):
                re, im = turned[k]
                if k > 0:
                    c, sn = real[pl.ds(TURN + k, 1), :], real[pl.ds(TURN + RAD + k, 1), :]
                    re, im = re * c + im * sn, im * c - re * sn
                re_h, im_h = re.astype(BF), im.astype(BF)
                re_l = (re - re_h.astype(F32)).astype(BF)
                im_l = (im - im_h.astype(F32)).astype(BF)
                for ref, r, i in ((yh, re_h, im_h), (yl, re_l, im_l)):
                    ref[s % 2, k, rows, 0:LEN] = r
                    ref[s % 2, k, rows, LEN : 2 * LEN] = i
                    ref[s % 2, k, low_rows, 0:LEN] = i
                    ref[s % 2, k, low_rows, LEN : 2 * LEN] = -r

    def dot_nt(a, b):
        return lax.dot_general(a, b, (((1,), (1,)), ((), ())), preferred_element_type=F32)

    def channels(chunk, *parts):
        @pl.loop(0, NY)
        def _(yd):
            k = yd * KK + chunk % KK
            for s in parts:
                high, low = yh[s, k], yl[s, k]
                o = dot_nt(table[0:LEN], high) + dot_nt(table[LEN : 2 * LEN], high) + dot_nt(table[0:LEN], low)
                b1[chunk, pl.ds(yd * NXC, NXC), s] = o.astype(BF).reshape(NXC, 16, LEN)

    def trade(first, count, sem):
        some = pl.ds(first, count)
        pltpu.make_async_copy(b1.at[some, me_xy], r1.at[some, me_xy], sem).start()

        @pl.loop(1, PLANE)
        def _(j):
            to = (me_xy + j) % PLANE
            pltpu.make_async_remote_copy(
                src_ref=b1.at[some, to],
                dst_ref=r1.at[some, me_xy],
                send_sem=xy_send,
                recv_sem=sem,
                device_id=at_xy(to),
                device_id_type=MESH,
            ).start()

    def traded(first, count, sem):
        here = r1.at[pl.ds(first, count)]
        pltpu.make_async_copy(here, here, sem).wait()

    def spread(chunk):
        @pl.loop(0, NY)
        def _(yd):
            rows = r1[chunk, pl.ds(yd * NXC, NXC)].reshape(256, LEN)
            o = jnp.dot(table[2 * LEN : 4 * LEN], rows, preferred_element_type=F32).astype(BF)
            zs[chunk, :, :, yd] = o.reshape(NZL, 2, 16, LEN)

    def send(chunks, part, sem, to):
        pltpu.make_async_remote_copy(
            src_ref=zs.at[(chunks, to % NZL, *part)],
            dst_ref=zr.at[(chunks, me_z, *part)],
            send_sem=z_send,
            recv_sem=sem,
            device_id=at_z(to),
            device_id_type=MESH,
        ).start()

    def pass_on(first, count, sem):
        some = pl.ds(first, count)
        pltpu.make_async_copy(zs.at[some, zl], zr.at[some, me_z], sem).start()

        @pl.loop(1, NZ)
        def _(j):
            send(some, (), sem, (me_z + NZ // 2 + (j // 2) * (1 - 2 * (j % 2)) * (1 - 2 * core) + NZ) % NZ)

    def pass_last(chunk, sems):
        for half in range(2):
            pltpu.make_async_copy(zs.at[chunk, zl, half], zr.at[chunk, me_z, half], sems[half]).start()
        for lo, hi in ((0, 4), (4, NZ)):
            for half in range(2):

                @pl.loop(lo, hi)
                def _(j, lo=lo, hi=hi, half=half):
                    to = j + core * (hi + lo - 1 - 2 * j)

                    @pl.when(to != me_z)
                    def _():
                        send(chunk, (half,), sems[half], to)

    def arrived(sem, chunks, *half):
        here = zr.at[(chunks, slice(None), *half)]
        pltpu.make_async_copy(here, here, sem).wait()

    def some(first, count, step):
        pl.loop(first, first + count)(step)

    spectrum(3)
    some(0, KK, lambda chunk: channels(chunk, 1))
    wait_halo(2)
    send_halo(2, 1)
    send_halo(1, 0)
    spectrum(2)
    channels(0, 0)
    trade(0, 1, xy_recv.at[0])
    traded(0, 1, xy_recv.at[0])
    spread(0)
    pass_on(0, 1, z_recv.at[0])
    some(1, KK - 1, lambda chunk: channels(chunk, 0))
    trade(1, KK - 1, xy_recv.at[1])
    traded(1, KK - 1, xy_recv.at[1])
    some(1, KK - 1, spread)
    pass_on(1, KK - 1, z_recv.at[1])
    wait_halo(1)
    spectrum(1)
    wait_halo(0)
    spectrum(0)
    some(KK, KK, lambda chunk: channels(chunk, 0, 1))
    trade(KK, KK, xy_recv.at[2])
    traded(KK, KK, xy_recv.at[2])
    some(KK, KK, spread)
    pass_on(KK, 2, z_recv.at[2])
    pass_on(KK + 2, 1, z_recv.at[3])
    pass_last(CHUNKS - 1, (z_recv.at[4], z_recv.at[5]))

    lane = lax.broadcasted_iota(jnp.int32, (IN_DEV, LEN), 1)
    scale = 1.0 / (CHAN * SPEC)
    sign = jnp.where(lane < IN_DEV, scale, -scale).astype(F32)

    def correlate(half, kk):
        for g in range(STN + LAGS - 1):
            st = (zh + g) % STN
            for sp in range(2):
                part = zr[sp * KK + kk, pl.ds((st % NZH) * NZL, NZL), half, st // NZH]
                gw[pl.ds(sp * 128, 128), pl.ds(g * LEN, LEN)] = part.reshape(128, LEN)
        slot = half * KK + kk
        ch = half * RAD + y * KK + kk

        def products(to):
            at = pl.multiple_of(2 * to * LEN, LEN)
            prod = lax.dot_general(
                gw[:, pl.ds(at, LEN)],
                gw[:, pl.ds(at, LAGS * LEN)],
                (((0,), (0,)), ((), ())),
                preferred_element_type=F32,
            )
            for lag in range(LAGS):
                top = prod[:IN_DEV, lag * LEN : (lag + 1) * LEN]
                low = prod[IN_DEV:, lag * LEN : (lag + 1) * LEN]
                whole = top * sign + pltpu.roll(low, IN_DEV, 1) * scale
                ob[slot, to, lag] = whole.astype(BF)

        @pl.loop(0, NY - 1)
        def _(j):
            to = (y + (j + 1) % (NY - 1) + 1) % NY
            products(to)
            pltpu.make_async_remote_copy(
                src_ref=ob.at[slot, to],
                dst_ref=out_ref.at[ch],
                send_sem=o_send,
                recv_sem=o_recv,
                device_id={"chan": chan, "stn": to * NZH + zh},
                device_id_type=MESH,
            ).start()

        products(y)
        pltpu.make_async_copy(ob.at[slot, y], out_ref.at[ch], o_recv).start()

    def both(kk):
        pl.loop(0, 2)(lambda half: correlate(half, kk))

    arrived(z_recv.at[0], 0)
    arrived(z_recv.at[1], pl.ds(1, KK - 1))
    arrived(z_recv.at[2], pl.ds(KK, 2))
    some(0, 2, both)
    arrived(z_recv.at[3], KK + 2)
    both(2)
    for half in range(2):
        arrived(z_recv.at[4 + half], CHUNKS - 1, half)
        correlate(half, KK - 1)

    pltpu.make_async_copy(out_ref, out_ref, o_recv).wait()

    @pl.when(chan < CHAN - 1)
    def _():
        for slot in range(3):
            pltpu.make_async_copy(halo.at[slot], halo.at[slot], halo_send.at[slot]).wait()

    sent = b1.at[:, pl.ds(0, PLANE - 1)]
    pltpu.make_async_copy(sent, sent, xy_send).wait()
    sent = zr.at[:, pl.ds(0, NZ - 1)]
    pltpu.make_async_copy(sent, sent, z_send).wait()
    sent = ob.at[:, pl.ds(0, NY - 1)]
    pltpu.make_async_copy(sent, sent, o_send).wait()


def finish(src, dst, held, sems, more):
    parts = [pl.ds(8 * i, 8) for i in range(4)]
    for i, part in enumerate(parts):
        pltpu.make_async_copy(src.at[part], held.at[part], sems.at[i]).start()
    for i, part in enumerate(parts):
        pltpu.make_async_copy(src.at[part], held.at[part], sems.at[i]).wait()
        pltpu.make_async_copy(held.at[part], dst.at[part], more.at[i]).start()
    for i, part in enumerate(parts):
        pltpu.make_async_copy(held.at[part], dst.at[part], more.at[i]).wait()


def local(voltages):
    dma = pltpu.SemaphoreType.DMA
    products = pl.pallas_call(
        kernel,
        out_shape=jax.ShapeDtypeStruct((2 * RAD, LAGS, IN_DEV, LEN), BF),
        in_specs=[pl.BlockSpec(memory_space=pl.ANY)] * 3,
        out_specs=pl.BlockSpec(memory_space=pl.ANY),
        scratch_shapes=[
            pltpu.VMEM((2, IN_DEV, SPEC * NCH), BF),
            pltpu.VMEM((TURN + 2 * RAD, LEN), F32),
            pltpu.VMEM((4 * LEN, 2 * LEN), BF),
            pltpu.VMEM((3, 2, IN_DEV, NCH), BF),
            pltpu.VMEM((2, RAD, 2 * IN_DEV, 2 * LEN), BF),
            pltpu.VMEM((2, RAD, 2 * IN_DEV, 2 * LEN), BF),
            pltpu.VMEM((CHUNKS, PLANE, 2, 16, LEN), BF),
            pltpu.VMEM((CHUNKS, PLANE, 2, 16, LEN), BF),
            pltpu.VMEM((CHUNKS, NZL, 2, NY, 16, LEN), BF),
            pltpu.VMEM((CHUNKS, NZ, 2, NY, 16, LEN), BF),
            pltpu.VMEM((256, (STN + LAGS - 1) * LEN), BF),
            pltpu.VMEM((2 * KK, NY, LAGS, IN_DEV, LEN), BF),
            dma((3,)),
            dma((3,)),
            dma((3,)),
            dma,
            dma((3,)),
            dma,
            dma((6,)),
            dma,
            dma,
        ],
        compiler_params=pltpu.CompilerParams(
            collective_id=0, has_side_effects=True, vmem_limit_bytes=60 * 2**20
        ),
    )(voltages, *(jnp.asarray(t) for t in tables()))
    products = pl.pallas_call(
        finish,
        out_shape=jax.ShapeDtypeStruct((2 * RAD, LAGS, IN_DEV, LEN), BF),
        in_specs=[pl.BlockSpec(memory_space=pl.ANY)],
        out_specs=pl.BlockSpec(memory_space=pl.ANY),
        scratch_shapes=[pltpu.VMEM((2 * RAD, LAGS, IN_DEV, LEN), BF), dma((4,)), dma((4,))],
        compiler_params=pltpu.CompilerParams(vmem_limit_bytes=60 * 2**20),
    )(products)
    return jnp.transpose(products, (0, 2, 1, 3))


def solution(mesh):
    return jax.shard_map(
        local,
        mesh=mesh,
        in_specs=(P(None, "stn", "chan"),),
        out_specs=P("chan", "stn", None, None),
        check_vma=False,
    )
```
